128 devices in a mesh: gx: 16 (over y, z), gy: 8 (over x, core).
Axes of the slice: x: 4, y: 4, z: 4, core: 2. Of those that a mesh axis runs over, the one named last changes fastest.
Arguments:
- ensemble: float32 [80, 1048576], P(None, ('gx', 'gy')), may hold values from -6 to 6
- measured_line_locations: int32 [4, 2048], P(None, ('gx', 'gy')), may hold values from 0 to 8191
- obs_values: float32 [4, 2048], P(None, ('gx', 'gy')), may hold values from -8 to 8
- obs_error: float32 [4, 2048], P(None, ('gx', 'gy')), may hold values from 0.3 to 3
- obs_count: int32 [4, 128], P(None, ('gx', 'gy')), may hold values from 5 to 16, as said below
- obs_blocks: int32 [4, 8, 2048], replicated, may hold values from 0 to 1023, as said below
- loc_weights: float32 [4, 8, 2048], replicated, may hold values from 0.1 to 1
Outputs:
- posterior: float32 [80, 1048576], P(None, ('gx', 'gy'))
The draws below stay inside these ranges and needn't reach their ends.
Inputs may be any that keep to these rules, and one draw needn't show every extreme that they name: `obs_count`: live slots of a device in a batch; slots from this count on are padding. In every batch some device has all 16 slots live. `obs_blocks`: block s holds global rows s * 1024 to s * 1024 + 1023. Every block in the list of an observation of device (i, j) lies on one of the devices (i + a mod 16, j + c mod 8) with a, c in -1, 0, 1 (periodic along both axes); entry 0 lies on the owning device. Entries may repeat.
All inputs are finite; a program needn't handle non-finite values.
Results may differ from the reference program's by a relative error of at most 0.0001.
Values sent between devices are 32-bit elements; how exact they have to be, the bound alone decides.
No kernel may reach another device: no remote copies, remote signals or barrier semaphores. Data moves between devices by JAX's collectives and lax.ppermute only.
A program may use at most 64 MiB of HBM per device.

```python
import math
import jax
import jax.numpy as jnp
from jax import lax

MEM = 80
ROWS_DEV = 8192
BLK = 1024
OBS_DEV = 16
NLIST = 8
BATCHES = 4
NROWS = 1048576
NBLK = 1024
NOBS = 2048
N_GX = 16
N_GY = 8


def draw_obs_count(key, part):
    key = jax.random.fold_in(key, 11)
    ndevices = N_GX * N_GY
    first, second, third = jax.random.split(key, 3)
    counts = jax.random.randint(first, (BATCHES, ndevices), OBS_DEV // 3, OBS_DEV + 1)
    fullest = jax.random.randint(second, (BATCHES,), 0, ndevices)
    offset = jax.random.randint(third, (BATCHES,), 1, ndevices)
    emptiest = (fullest + offset) % ndevices
    column = jnp.arange(ndevices, dtype=jnp.int32)[None, :]
    counts = jnp.where(column == fullest[:, None], OBS_DEV, counts)
    counts = jnp.where(column == emptiest[:, None], OBS_DEV // 3, counts)
    return counts.astype(jnp.int32)


def draw_obs_blocks(key, part):
    key = jax.random.fold_in(key, 23)
    first, second, third = jax.random.split(key, 3)
    owners = jnp.arange(NOBS, dtype=jnp.int32) // OBS_DEV
    owner_x = owners // N_GY
    owner_y = owners % N_GY
    step_x = jax.random.randint(first, (BATCHES, NLIST, NOBS), -1, 2)
    step_y = jax.random.randint(second, (BATCHES, NLIST, NOBS), -1, 2)
    entry = jnp.arange(NLIST, dtype=jnp.int32)[None, :, None]
    step_x = jnp.where(entry == 0, 0, step_x)
    step_y = jnp.where(entry == 0, 0, step_y)
    near_x = (owner_x[None, None, :] + step_x) % N_GX
    near_y = (owner_y[None, None, :] + step_y) % N_GY
    local = jax.random.randint(third, (BATCHES, NLIST, NOBS), 0, ROWS_DEV // BLK)
    return ((near_x * N_GY + near_y) * (ROWS_DEV // BLK) + local).astype(jnp.int32)


def plant(drawn, stream_key, least, largest):
    longest = drawn.shape.index(max(drawn.shape))
    spots = []
    for shift in (0, 1):
        where = [jax.random.randint(jax.random.fold_in(stream_key, axis), (), 0, length) for axis, length in enumerate(drawn.shape)]
        where[longest] = (where[longest] + shift) % drawn.shape[longest]
        spots.append(tuple(where))
    return drawn.at[spots[0]].set(least).at[spots[1]].set(largest)


def shard_levels(key, dims, pieces, low, largest):
    def one(dim, blocks):
        draws = jax.random.uniform(jax.random.fold_in(jax.random.fold_in(key, 6), dim), (blocks,), jnp.float32, low / len(pieces), largest / len(pieces))
        return jnp.repeat(jnp.exp(draws), dims[dim] // blocks).reshape((-1,) + (1,) * (len(dims) - dim - 1))

    factor_of = one(*pieces[0])
    for cut in pieces[1:]:
        factor_of = factor_of * one(*cut)
    return factor_of


def bell_draw(key, shape, width, most, cuts=(), kind=jnp.bfloat16):
    drawn = width * jax.random.normal(key, shape, jnp.float32)
    if cuts:
        drawn = drawn * shard_levels(key, shape, cuts, -0.22, 0.18)
    return jnp.clip(drawn, -most, most).astype(kind)


def setup_inputs(seed: int = 0) -> dict:
    seeds = jax.random.split(jax.random.key(seed), 8)
    ensemble = bell_draw(seeds[0], (MEM, NROWS), 1.0, 6.0, ((1, 128),), jnp.float32)
    measured_line_locations = plant(jax.random.randint(seeds[1], (BATCHES, NOBS), 0, ROWS_DEV), jax.random.fold_in(seeds[1], 1), 0, ROWS_DEV - 1).astype(jnp.int32)
    obs_values = bell_draw(seeds[2], (BATCHES, NOBS), 1.5, 8.0, ((1, 128),), jnp.float32)
    obs_error = jnp.clip(jnp.exp(math.log(3.0) - 2.3025851 * jax.random.uniform(seeds[3], (BATCHES, NOBS), jnp.float32) ** shard_levels(seeds[3], (BATCHES, NOBS), ((1, 128),), -0.2, 0.2)), 0.3, 3.0)
    obs_count = draw_obs_count(jax.random.fold_in(seeds[7], 71), 0)
    obs_blocks = draw_obs_blocks(jax.random.fold_in(seeds[7], 71), 0)
    loc_weights = jnp.clip(jax.random.uniform(seeds[6], (BATCHES, NLIST, NOBS), jnp.float32, 0.1, 1.0), 0.1, 1.0)
    return dict(ensemble=ensemble, measured_line_locations=measured_line_locations, obs_values=obs_values, obs_error=obs_error, obs_count=obs_count, obs_blocks=obs_blocks, loc_weights=loc_weights)


EPS = 1e-05

def reference(ensemble, measured_line_locations, obs_values, obs_error, obs_count, obs_blocks, loc_weights):
    present_sweep_value = ensemble
    slots = jnp.arange(NOBS, dtype=jnp.int32)
    owners = slots // OBS_DEV
    within = slots % OBS_DEV
    for group_of_sets in range(BATCHES):
        line_entries = measured_line_locations[group_of_sets] + owners * ROWS_DEV
        predicted_measurement = jnp.take(present_sweep_value, line_entries, axis=1)
        prior_average = lax.optimization_barrier(jnp.mean(predicted_measurement, axis=0))
        measured_spread_vector = predicted_measurement - prior_average
        obs_var = lax.optimization_barrier(jnp.sum(measured_spread_vector * measured_spread_vector, axis=0)) / (MEM - 1) + EPS
        error = obs_error[group_of_sets]
        increment = obs_var / (obs_var + error) * (obs_values[group_of_sets] - prior_average) + (jnp.sqrt(error / (obs_var + error)) - 1.0) * measured_spread_vector
        live = (within < jnp.take(obs_count[group_of_sets], owners)).astype(jnp.float32)
        scaled = measured_spread_vector * (live / ((MEM - 1) * obs_var))

        def add_entry(total, entry):
            blocks, weights = entry
            outer = jnp.einsum('ko,mo->okm', scaled * weights, increment, precision=lax.Precision.HIGHEST)
            return (total + jax.ops.segment_sum(outer, blocks, num_segments=NBLK), None)
        kalman_gain_factor, unused = lax.scan(add_entry, jnp.zeros((NBLK, MEM, MEM), jnp.float32), (obs_blocks[group_of_sets], loc_weights[group_of_sets]))
        member_deviation = (present_sweep_value - lax.optimization_barrier(jnp.mean(present_sweep_value, axis=0))).reshape(MEM, NBLK, BLK)
        state_adjust = jnp.einsum('bnt,nbf->tbf', kalman_gain_factor, member_deviation, precision=lax.Precision.HIGHEST)
        present_sweep_value = present_sweep_value + state_adjust.reshape(MEM, NROWS)
    return present_sweep_value
```

```python
import jax
import jax.numpy as jnp
from jax import lax
from jax.experimental import pallas as pl
from jax.experimental.pallas import tpu as pltpu
from jax.sharding import PartitionSpec as P

BLK = 1024
BATCHES = 4
EPS = 1e-05
F32 = jnp.float32
BF16 = jnp.bfloat16
VMEM = pltpu.VMEM
SMEM = pltpu.SMEM
NT = (((1,), (1,)), ((), ()))
NN = (((1,), (0,)), ((), ()))
TN = (((0,), (0,)), ((), ()))


def split(x):
    high = x.astype(BF16)
    return high, (x - high.astype(F32)).astype(BF16)


def dot3(a, b, dims):
    ah, al = a
    bh, bl = b
    d = lambda p, q: lax.dot_general(p, q, dims, preferred_element_type=F32)
    return d(ah, bh) + (d(ah, bl) + d(al, bh))


def column(row, slots):
    i = lax.broadcasted_iota(jnp.int32, (slots, slots), 0)
    j = lax.broadcasted_iota(jnp.int32, (slots, slots), 1)
    return jnp.sum(jnp.where(i == j, row, jnp.zeros_like(row)), axis=1, keepdims=True)


def message(measured, values, error, count):
    slots, members = measured.shape
    mean = jnp.sum(measured, axis=1, keepdims=True) / members
    anomaly = measured - mean
    var = jnp.sum(anomaly * anomaly, axis=1, keepdims=True) / (members - 1) + EPS
    error = column(error, slots)
    values = column(values, slots)
    increment = (
        var / (var + error) * (values - mean) + (jnp.sqrt(error / (var + error)) - 1.0) * anomaly
    )
    live = (lax.broadcasted_iota(jnp.int32, (slots, 1), 0) < count).astype(F32)
    scaled = anomaly * (live / ((members - 1) * var))
    scaled = scaled - jnp.sum(scaled, axis=1, keepdims=True) / members
    return scaled, increment


def gather_kernel(loc, count, ens, values, error, measured, msg):
    members = ens.shape[0]
    batches, slots = loc.shape
    lane = lax.broadcasted_iota(jnp.int32, (members, 128), 1)
    acc = jnp.zeros((members, 128), F32)
    for j in range(batches * slots):
        c = loc[j // slots, j % slots]
        tile = ens[:, pl.ds(pl.multiple_of((c // 128) * 128, 128), 128)]
        acc = jnp.where(lane == j, pltpu.roll(tile, (j - c % 128 + 128) % 128, 1), acc)
    rows = jnp.transpose(acc)[: batches * slots]
    measured[...] = rows
    scaled, increment = message(rows[:slots], values[0:1, :], error[0:1, :], count[0, 0])
    msg[:slots] = scaled
    msg[slots:] = increment


def coef_kernel(loc, place, blocks, weights, coef, col_coef):
    batches, slots = loc.shape
    nb = coef.shape[1]
    lane = lax.broadcasted_iota(jnp.int32, (nb, 128), 1)
    row = lax.broadcasted_iota(jnp.int32, (nb, 128), 0)
    first = place[3] * nb
    north = place[4]
    span = 3 * slots
    for b in range(batches):
        lo = jnp.zeros((nb, 128), F32)
        hi = jnp.zeros((nb, 128), F32)
        for a in range(3):
            at = pl.ds(pl.multiple_of(place[a] * 128, 128), 128)
            bl = blocks[b, :, at] - first
            w = weights[b, :, at]
            tile = jnp.zeros((nb, 128), F32)
            for s in range(nb):
                one = jnp.sum(jnp.where(bl == s, w, 0.0), axis=0, keepdims=True)
                tile = jnp.where(row == s, one, tile)
            tile = pltpu.roll(tile, (a * span - (north - 1) * slots + 256) % 128, 1)
            keep = (lane >= a * span) & (lane < (a + 1) * span)
            lo = jnp.where(keep, tile, lo)
            over = (a + 1) * span - 128
            if over > 0:
                hi = jnp.where(lane < over, tile, hi)
        coef[b, :, 0:128] = lo
        coef[b, :, 128:256] = hi
    for b in range(batches - 1):
        for r in range((b + 1) * slots, batches * slots):
            s = loc[r // slots, r % slots] // BLK
            col_coef[b, r : r + 1, :] = coef[b, pl.ds(s, 1), :]


def near(groups, slots):
    scaled = [g[k * 2 * slots : k * 2 * slots + slots] for g in groups for k in range(3)]
    increment = [g[k * 2 * slots + slots : (k + 1) * 2 * slots] for g in groups for k in range(3)]
    return split(jnp.concatenate(scaled, axis=0)), split(jnp.concatenate(increment, axis=0))


def step_kernel(batch, count, west, here, east, measured, col_coef, values, error, out, msg):
    slots = values.shape[1]
    scaled, increment = near((west[...], here[...], east[...]), slots)
    nobs = scaled[0].shape[0]
    begin = (batch + 1) * slots
    rows = measured[begin:]
    s = dot3(split(rows), scaled, NT)
    p = s * col_coef[batch, begin:, :nobs]
    rows = rows + dot3(split(p), increment, NN)
    out[begin:] = rows
    b = batch + 1
    scaled, increment = message(rows[:slots], values[b : b + 1, :], error[b : b + 1, :], count[b, 0])
    msg[:slots] = scaled
    msg[slots:] = increment


def map_kernel(batch, slots, west, here, east, coef, maps, out):
    nb = coef.shape[1]
    members = west.shape[1]
    scaled, increment = near((west[...], here[...], east[...]), slots)
    nobs = scaled[0].shape[0]
    i = lax.broadcasted_iota(jnp.int32, (members, members), 0)
    j = lax.broadcasted_iota(jnp.int32, (members, members), 1)
    for k in range(nb):
        e = jnp.where(i == j, 1.0, 0.0) if maps is None else maps[k]
        s = dot3(split(e), scaled, NT)
        p = s * coef[batch, k : k + 1, :nobs]
        out[k] = e + dot3(split(p), increment, NN)


def final_kernel(batch, slots, west, here, east, coef, maps, ens, out):
    members = west.shape[1]
    scaled, increment = near((west[...], here[...], east[...]), slots)
    nobs = scaled[0].shape[0]
    i = lax.broadcasted_iota(jnp.int32, (members, members), 0)
    j = lax.broadcasted_iota(jnp.int32, (members, members), 1)
    e = maps[0]
    s = dot3(split(e), scaled, NT)
    p = s * coef[batch, pl.ds(pl.program_id(0), 1), :nobs]
    d = e - jnp.where(i == j, 1.0, 0.0) + dot3(split(p), increment, NN)
    dh, dl = split(d)
    x = ens[...]
    xh, xl = split(x)
    left = jnp.concatenate([dh, dl, dh], axis=0)
    right = jnp.concatenate([xh, xh, xl], axis=0)
    out[...] = x + lax.dot_general(left, right, TN, preferred_element_type=F32)


def shift(x, axis, step):
    n = lax.axis_size(axis)
    return lax.ppermute(x, axis, [(i, (i + step) % n) for i in range(n)])


def shards(ensemble, loc, values, error, count, blocks, weights):
    members, rows_here = ensemble.shape
    batches, slots = loc.shape
    nb = rows_here // BLK
    nx, ny = lax.axis_size("gx"), lax.axis_size("gy")
    ix, iy = lax.axis_index("gx"), lax.axis_index("gy")
    vm = pl.BlockSpec(memory_space=VMEM)
    sm = pl.BlockSpec(memory_space=SMEM)
    params = pltpu.CompilerParams(vmem_limit_bytes=32 * 1024 * 1024)
    shape = lambda *s: jax.ShapeDtypeStruct(s, F32)
    nrows = batches * slots

    measured, msg = pl.pallas_call(
        gather_kernel,
        out_shape=(shape(nrows, members), shape(2 * slots, members)),
        in_specs=[sm, sm, vm, vm, vm],
        out_specs=(vm, vm),
        compiler_params=params,
        name="gather_columns",
    )(loc, count, ensemble, values, error)

    place = jnp.stack([(ix + nx - 1) % nx, ix, (ix + 1) % nx, ix * ny + iy, iy]).astype(jnp.int32)
    coef, col_coef = pl.pallas_call(
        coef_kernel,
        out_shape=(shape(batches, nb, 256), shape(batches - 1, nrows, 256)),
        in_specs=[sm, sm, vm, vm],
        out_specs=(vm, vm),
        compiler_params=params,
        name="list_coefficients",
    )(loc, place, blocks, weights)

    maps = None
    for b in range(batches):
        south, north = shift(msg, "gy", 1), shift(msg, "gy", -1)
        line = jnp.concatenate([south, msg, north], axis=0)
        halo = (shift(line, "gx", 1), line, shift(line, "gx", -1))
        if b < batches - 1:
            measured, msg = pl.pallas_call(
                lambda *refs, b=b: step_kernel(b, *refs),
                out_shape=(shape(nrows, members), shape(2 * slots, members)),
                in_specs=[sm] + [vm] * 7,
                out_specs=(vm, vm),
                compiler_params=params,
                name="step_columns",
            )(count, *halo, measured, col_coef, values, error)
            given = () if maps is None else (maps,)
            body = (
                (lambda w, h, e, c, o, b=b: map_kernel(b, slots, w, h, e, c, None, o))
                if maps is None
                else (lambda w, h, e, c, m, o, b=b: map_kernel(b, slots, w, h, e, c, m, o))
            )
            maps = pl.pallas_call(
                body,
                out_shape=shape(nb, members, members),
                in_specs=[vm] * (4 + len(given)),
                out_specs=vm,
                compiler_params=params,
                cost_estimate=pl.CostEstimate(flops=10**9, bytes_accessed=10**6, transcendentals=0),
                name="compose_maps",
            )(*halo, coef, *given)
        else:
            posterior = pl.pallas_call(
                lambda *refs, b=b: final_kernel(b, slots, *refs),
                out_shape=shape(members, rows_here),
                grid=(nb,),
                in_specs=[vm] * 4
                + [
                    pl.BlockSpec((1, members, members), lambda k: (k, 0, 0)),
                    pl.BlockSpec((members, BLK), lambda k: (0, k)),
                ],
                out_specs=pl.BlockSpec((members, BLK), lambda k: (0, k)),
                compiler_params=params,
                name="apply_maps",
            )(*halo, coef, maps, ensemble)
    return posterior


def solution(mesh):
    split_specs = P(None, ("gx", "gy"))
    in_specs = (split_specs,) * 5 + (P(), P())
    return jax.shard_map(
        shards, mesh=mesh, in_specs=in_specs, out_specs=split_specs, check_vma=False
    )
```

```python
import jax
import jax.numpy as jnp
from jax import lax
from jax.experimental import pallas as pl
from jax.experimental.pallas import tpu as pltpu
from jax.sharding import PartitionSpec as P

BLK = 1024
EPS = 1e-05
ZN = 4
PAD = 8
F32 = jnp.float32
BF16 = jnp.bfloat16
VMEM = pltpu.VMEM
NT = (((1,), (1,)), ((), ()))
NN = (((1,), (0,)), ((), ()))
TN = (((0,), (0,)), ((), ()))


def split(x):
    high = x.astype(BF16)
    return high, (x - high.astype(F32)).astype(BF16)


def dot3(a, b, dims):
    ah, al = a
    bh, bl = b
    d = lambda p, q: lax.dot_general(p, q, dims, preferred_element_type=F32)
    return d(ah, bh) + (d(ah, bl) + d(al, bh))


def observe(rows):
    members = rows.shape[1] - PAD
    x = rows[:, :members]
    value, error, live = (rows[:, members + k : members + k + 1] for k in (1, 2, 3))
    mean = jnp.sum(x, axis=1, keepdims=True) / members
    anomaly = x - mean
    var = jnp.sum(anomaly * anomaly, axis=1, keepdims=True) / (members - 1) + EPS
    increment = (
        var / (var + error) * (value - mean) + (jnp.sqrt(error / (var + error)) - 1.0) * anomaly
    )
    centred = anomaly - jnp.sum(anomaly, axis=1, keepdims=True) / members
    return centred * (live / ((members - 1) * var)), increment


def width(batch, batches):
    return 2 * (batches - batch) + 1


def gather_kernel(loc_in, count_in, value_in, error_in, ens_in, out, loc, count, values, error, ens, sems):
    members = ens.shape[0]
    batches, slots = loc.shape
    n = batches * slots
    small = [(loc_in, loc), (count_in, count), (value_in, values), (error_in, error)]
    copies = [pltpu.make_async_copy(src, dst, sems.at[k]) for k, (src, dst) in enumerate(small)]
    for k in range(ens.shape[1] // BLK):
        at = pl.ds(k * BLK, BLK)
        copies.append(pltpu.make_async_copy(ens_in.at[:, at], ens.at[:, at], sems.at[4 + k]))
    for copy in copies:
        copy.start()
    device = lax.axis_index("gx") * lax.axis_size("gy") + lax.axis_index("gy")
    first = device * (ens.shape[1] // BLK)
    lane = lax.broadcasted_iota(jnp.int32, (members, 128), 1)
    lane8 = lax.broadcasted_iota(jnp.int32, (PAD, 128), 1)
    row8 = lax.broadcasted_iota(jnp.int32, (PAD, 128), 0)
    side = jnp.zeros((PAD, 128), F32)
    for copy in copies[:4]:
        copy.wait()
    for j in range(n):
        b, k = j // slots, j % slots
        block = (first + loc[b, k] // BLK).astype(F32)
        live = jnp.where(k < count[0, b], 1.0, 0.0).astype(F32)
        new = jnp.where(
            row8 == 0, block, jnp.where(row8 == 1, values[b, k], jnp.where(row8 == 2, error[b, k], live))
        )
        side = jnp.where(lane8 == j, new, side)
    for copy in copies[4:]:
        copy.wait()
    acc = jnp.zeros((members, 128), F32)
    for j in range(n):
        c = loc[j // slots, j % slots]
        tile = ens[:, pl.ds(pl.multiple_of((c // 128) * 128, 128), 128)]
        acc = jnp.where(lane == j, pltpu.roll(tile, (j - c % 128 + 128) % 128, 1), acc)
    out[...] = jnp.transpose(jnp.concatenate([acc, side], axis=0))[:n]


def pack_kernel(blocks, weights, list_blocks, list_weights, coef):
    batches, nlist = blocks.shape[:2]
    nb = coef.shape[1]
    lanes = list_blocks.shape[2]
    nx, ny = lax.axis_size("gx"), lax.axis_size("gy")
    ix, iy = lax.axis_index("gx"), lax.axis_index("gy")
    slots = blocks.shape[2] // (nx * ny)
    row_lanes = ny * slots
    first = (ix * ny + iy) * nb
    span = 3 * slots
    lane = lax.broadcasted_iota(jnp.int32, (nlist, 128), 1)
    row = lax.broadcasted_iota(jnp.int32, (nb, 128), 0)
    for b in range(batches):
        w = width(b, batches)
        held_b = [jnp.full((nlist, 128), -1, jnp.int32) for _ in range(lanes // 128)]
        held_w = [jnp.zeros((nlist, 128), F32) for _ in range(lanes // 128)]
        held_c = [jnp.zeros((nb, 128), F32) for _ in range(2)]

        def put(held, tile, d):
            tile = pltpu.roll(tile, (d * span - (iy - 1) * slots + 4 * 128) % 128, 1)
            begin, end = d * span, (d + 1) * span
            for t in range(begin // 128, (end - 1) // 128 + 1):
                keep = (lane >= begin - t * 128) & (lane < end - t * 128)
                held[t] = jnp.where(keep, tile, held[t])

        for d in range(w):
            near = (ix + d - w // 2 + nx) % nx
            at = pl.ds(pl.multiple_of(near * row_lanes, row_lanes), row_lanes)
            bl, wt = blocks[b, :, at], weights[b, :, at]
            put(held_b, bl, d)
            put(held_w, wt, d)
            if abs(d - w // 2) <= 1:
                tile = jnp.zeros((nb, 128), F32)
                for s in range(nb):
                    one = jnp.sum(jnp.where(bl == first + s, wt, 0.0), axis=0, keepdims=True)
                    tile = jnp.where(row == s, one, tile)
                put(held_c, tile, d - w // 2 + 1)
        for t in range(lanes // 128):
            list_blocks[b, :, t * 128 : (t + 1) * 128] = held_b[t]
            list_weights[b, :, t * 128 : (t + 1) * 128] = held_w[t]
        for t in range(2):
            coef[b, :, t * 128 : (t + 1) * 128] = held_c[t]


def along_z_kernel(slots, own, south, north, across, up, down):
    z = lax.axis_index("gx") % ZN
    mine, below, above = own[...], south[...], north[...]
    n = mine.shape[0]
    up[:n] = jnp.where(z == ZN - 1, below, mine)
    up[n:] = jnp.where(z == ZN - 1, mine, above)[: 2 * slots]
    down[:n] = jnp.where(z == 0, above, mine)
    down[n:] = jnp.where(z == 0, mine, below)[: 2 * slots]
    across[: 3 * slots] = jnp.where(z < 2, mine, below)[: 3 * slots]
    across[3 * slots :] = jnp.where(z < 2, above, mine)[: 3 * slots]


def window_kernel(batches, slots, own, south, north, across, up, down, first, rest):
    n = batches * slots
    source = {
        0: (own, 0),
        -4: (south, 0),
        4: (north, 0),
        -1: (up, 0),
        3: (up, n),
        1: (down, 0),
        -3: (down, n),
        -2: (across, 0),
        2: (across, 3 * slots),
    }
    at = 0
    for b in range(batches):
        half = batches - b
        for d in range(-half, half + 1):
            ref, begin = source[d]
            piece = ref[begin + b * slots : begin + (b + 1) * slots]
            if b == 0:
                first[(d + half) * slots : (d + half + 1) * slots] = piece
            else:
                rest[at : at + slots] = piece
                at += slots


def gathered(own, swapped, crossed, slots):
    even = lax.axis_index("gy") % 2 == 0
    a, b, mine = swapped[...], crossed[...], own[...]
    south = jnp.where(even, b, a)
    north = jnp.where(even, a, b)
    pieces = []
    for d in range(mine.shape[0] // slots):
        at = slice(d * slots, (d + 1) * slots)
        pieces += [south[at], mine[at], north[at]]
    return jnp.concatenate(pieces, axis=0)


def mask_of(batch, rest, list_blocks, list_weights, nobs):
    members = rest.shape[1] - PAD
    block = rest[:, members : members + 1].astype(jnp.int32)
    lanes = (nobs + 127) // 128 * 128
    mask = jnp.zeros((rest.shape[0], lanes), F32)
    for l in range(list_blocks.shape[1]):
        mask = mask + jnp.where(
            block == list_blocks[batch, l : l + 1, :lanes], list_weights[batch, l : l + 1, :lanes], 0.0
        )
    return mask


def compose(batch, maps, scaled, increment, coef):
    nb = coef.shape[1]
    members = scaled.shape[1]
    nobs = scaled.shape[0]
    scaled, increment = split(scaled), split(increment)
    s = dot3(split(maps), scaled, NT)
    p = jnp.concatenate(
        [s[k * members : (k + 1) * members] * coef[batch, k : k + 1, :nobs] for k in range(nb)], axis=0
    )
    return maps + dot3(split(p), increment, NN)


def unit(members):
    i = lax.broadcasted_iota(jnp.int32, (members, members), 0)
    j = lax.broadcasted_iota(jnp.int32, (members, members), 1)
    return jnp.where(i == j, 1.0, 0.0).astype(F32)


def mask_kernel(batch, nobs, rest, list_blocks, list_weights, mask):
    mask[...] = mask_of(batch, rest[...], list_blocks, list_weights, nobs)


def map_kernel(batch, scaled, increment, coef, maps, out):
    nb = coef.shape[1]
    start = jnp.concatenate([unit(scaled.shape[1])] * nb, axis=0) if maps is None else maps[...]
    out[...] = compose(batch, start, scaled[...], increment[...], coef)


def step_kernel(slots, own, swapped, crossed, rest, mask, nxt, left, center_s, center_i):
    members = rest.shape[1] - PAD
    scaled, increment = observe(gathered(own, swapped, crossed, slots))
    nobs = scaled.shape[0]
    mid = nobs // (6 * slots) * 3 * slots
    center_s[...] = scaled[mid - 3 * slots : mid + 6 * slots]
    center_i[...] = increment[mid - 3 * slots : mid + 6 * slots]
    rows = rest[...]
    x = rows[:, :members]
    p = dot3(split(x), split(scaled), NT) * mask[:, :nobs]
    x = x + dot3(split(p), split(increment), NN)
    k = nxt.shape[0]
    nxt[:, :members] = x[:k]
    nxt[:, members:] = rows[:k, members:]
    if left is not None:
        left[:, :members] = x[k:]
        left[:, members:] = rows[k:, members:]


def final_kernel(batch, slots, own, swapped, crossed, coef, maps, ens, out, result, sems):
    nb = coef.shape[1]
    members = ens.shape[0]
    scaled, increment = observe(gathered(own, swapped, crossed, slots))
    whole = compose(batch, maps[...], scaled, increment, coef)
    eye = unit(members)
    copies = []
    for k in range(nb):
        dh, dl = split(whole[k * members : (k + 1) * members] - eye)
        x = ens[:, k * BLK : (k + 1) * BLK]
        xh, xl = split(x)
        left = jnp.concatenate([dh, dl, dh], axis=0)
        right = jnp.concatenate([xh, xh, xl], axis=0)
        at = pl.ds(k * BLK, BLK)
        result[:, at] = x + lax.dot_general(left, right, TN, preferred_element_type=F32)
        copies.append(pltpu.make_async_copy(result.at[:, at], out.at[:, at], sems.at[k]))
        copies[-1].start()
    for copy in copies:
        copy.wait()


def permute(x, target):
    nx, ny = lax.axis_size("gx"), lax.axis_size("gy")
    pairs = []
    for i in range(nx):
        for j in range(ny):
            a, c = target(i, j)
            pairs.append((i * ny + j, (a % nx) * ny + c % ny))
    return lax.ppermute(x, ("gx", "gy"), pairs)


def shards(ensemble, loc, values, error, count, blocks, weights):
    members, rows_here = ensemble.shape
    batches, slots = loc.shape
    nb = rows_here // BLK
    n = batches * slots
    wide = members + PAD
    vm = pl.BlockSpec(memory_space=VMEM)
    hbm = pl.BlockSpec(memory_space=pltpu.HBM)
    tie = pl.BlockSpec(memory_space=pl.ANY)
    params = pltpu.CompilerParams(vmem_limit_bytes=40 * 1024 * 1024)
    shape = lambda *s: jax.ShapeDtypeStruct(s, F32)
    cost = lambda us: pl.CostEstimate(flops=us * 10**6, bytes_accessed=us * 10**5, transcendentals=0)

    own = pl.pallas_call(
        gather_kernel,
        out_shape=shape(n, wide),
        in_specs=[hbm] * 5,
        out_specs=vm,
        scratch_shapes=[
            pltpu.SMEM((batches, slots), jnp.int32),
            pltpu.SMEM((1, batches), jnp.int32),
            pltpu.SMEM((batches, slots), F32),
            pltpu.SMEM((batches, slots), F32),
            pltpu.VMEM((members, rows_here), F32),
            pltpu.SemaphoreType.DMA((4 + nb,)),
        ],
        compiler_params=pltpu.CompilerParams(vmem_limit_bytes=64 * 1024 * 1024 - 2**21),
        name="gather_columns",
    )(loc, count.reshape(1, batches), values, error, ensemble)

    lanes = (width(0, batches) * 3 * slots + 127) // 128 * 128
    list_blocks, list_weights, coef = pl.pallas_call(
        pack_kernel,
        out_shape=(
            jax.ShapeDtypeStruct((batches, blocks.shape[1], lanes), jnp.int32),
            shape(batches, blocks.shape[1], lanes),
            shape(batches, nb, 256),
        ),
        in_specs=[vm, vm],
        out_specs=(vm, vm, vm),
        compiler_params=params,
        cost_estimate=cost(1),
        name="pack_lists",
    )(blocks, weights)

    south = permute(own, lambda i, j: (i + ZN, j))
    north = permute(own, lambda i, j: (i - ZN, j))
    across, up, down = pl.pallas_call(
        lambda *refs: along_z_kernel(slots, *refs),
        out_shape=(shape(6 * slots, wide), shape(n + 2 * slots, wide), shape(n + 2 * slots, wide)),
        in_specs=[vm] * 3,
        out_specs=(vm,) * 3,
        compiler_params=params,
        name="select_along_z",
    )(own, south, north)
    turn = lambda k: (lambda i, j: (i // ZN * ZN + (i + k) % ZN, j))
    across = permute(across, turn(2))
    up = permute(up, turn(1))
    down = permute(down, turn(ZN - 1))
    total = sum(width(b, batches) for b in range(1, batches)) * slots
    here, rest = pl.pallas_call(
        lambda *refs: window_kernel(batches, slots, *refs),
        out_shape=(shape(width(0, batches) * slots, wide), shape(total, wide)),
        in_specs=[vm] * 6,
        out_specs=(vm, vm),
        compiler_params=params,
        name="lay_out_window",
    )(own, south, north, across, up, down)

    maps = None
    for b in range(batches):
        swapped = permute(here, lambda i, j: (i, j + 1 - 2 * (j % 2)))
        crossed = permute(here, lambda i, j: (i, j + 1 if j % 2 else j - 1))
        if b > 0:
            given = () if maps is None else (maps,)
            body = lambda s, i, c, *r, b=b: map_kernel(b - 1, s, i, c, r[0] if len(r) == 2 else None, r[-1])
            maps = pl.pallas_call(
                body,
                out_shape=shape(nb * members, members),
                in_specs=[vm] * (3 + len(given)),
                out_specs=vm,
                compiler_params=params,
                cost_estimate=cost(1),
                name="compose_maps",
            )(center_s, center_i, coef, *given)
        if b == batches - 1:
            break
        w = width(b, batches)
        nobs = w * 3 * slots
        mask = pl.pallas_call(
            lambda *refs, b=b, nobs=nobs: mask_kernel(b, nobs, *refs),
            out_shape=shape(rest.shape[0], (nobs + 127) // 128 * 128),
            in_specs=[vm] * 3,
            out_specs=vm,
            compiler_params=params,
            cost_estimate=cost(1),
            name="list_mask",
        )(rest, list_blocks, list_weights)
        k = width(b + 1, batches) * slots
        outs = [shape(k, wide), shape(9 * slots, members), shape(9 * slots, members)]
        last = rest.shape[0] == k
        if not last:
            outs.insert(1, shape(rest.shape[0] - k, wide))
            body = lambda *refs: step_kernel(slots, *refs[:5], *refs[-4:])
        else:
            body = lambda *refs: step_kernel(slots, *refs[:5], refs[-3], None, *refs[-2:])
        after = () if maps is None else (maps,)
        res = pl.pallas_call(
            body,
            out_shape=tuple(outs),
            in_specs=[vm] * 5 + [tie] * len(after),
            out_specs=(vm,) * len(outs),
            compiler_params=params,
            name="step_columns",
        )(here, swapped, crossed, rest, mask, *after)
        here, center_s, center_i = res[0], res[-2], res[-1]
        rest = None if last else res[1]

    return pl.pallas_call(
        lambda *refs: final_kernel(batches - 1, slots, *refs),
        out_shape=shape(members, rows_here),
        in_specs=[vm] * 6,
        out_specs=hbm,
        scratch_shapes=[pltpu.VMEM((members, rows_here), F32), pltpu.SemaphoreType.DMA((nb,))],
        compiler_params=params,
        name="apply_maps",
    )(here, swapped, crossed, coef, maps, ensemble)


def solution(mesh):
    split_specs = P(None, ("gx", "gy"))
    in_specs = (split_specs,) * 5 + (P(), P())
    return jax.shard_map(
        shards, mesh=mesh, in_specs=in_specs, out_specs=split_specs, check_vma=False
    )
```

```python
import jax
import jax.numpy as jnp
from jax import lax
from jax.experimental import pallas as pl
from jax.experimental.pallas import tpu as pltpu
from jax.sharding import PartitionSpec as P

BLK = 1024
EPS = 1e-05
ZN = 4
SLAB = 16
PAD = 8
F32 = jnp.float32
BF16 = jnp.bfloat16
VMEM = pltpu.VMEM
NT = (((1,), (1,)), ((), ()))
NN = (((1,), (0,)), ((), ()))
TN = (((0,), (0,)), ((), ()))


def split(x):
    high = x.astype(BF16)
    return high, (x - high.astype(F32)).astype(BF16)


def dot3(a, b, dims):
    ah, al = a
    bh, bl = b
    d = lambda p, q: lax.dot_general(p, q, dims, preferred_element_type=F32)
    return d(ah, bh) + (d(ah, bl) + d(al, bh))


def observe(rows):
    members = rows.shape[1] - PAD
    x = rows[:, :members]
    value, error, live = (rows[:, members + k : members + k + 1] for k in (1, 2, 3))
    mean = jnp.sum(x, axis=1, keepdims=True) / members
    anomaly = x - mean
    var = jnp.sum(anomaly * anomaly, axis=1, keepdims=True) / (members - 1) + EPS
    increment = (
        var / (var + error) * (value - mean) + (jnp.sqrt(error / (var + error)) - 1.0) * anomaly
    )
    centred = anomaly - jnp.sum(anomaly, axis=1, keepdims=True) / members
    return centred * (live / ((members - 1) * var)), increment


def width(batch, batches):
    return 2 * (batches - batch) + 1


def gather_kernel(loc_in, count_in, value_in, error_in, ens_in, out, loc, count, values, error, ens, sems):
    members = ens.shape[0]
    batches, slots = loc.shape
    n = batches * slots
    small = [(loc_in, loc), (count_in, count), (value_in, values), (error_in, error)]
    copies = [pltpu.make_async_copy(src, dst, sems.at[k]) for k, (src, dst) in enumerate(small)]
    for k in range(members // SLAB):
        at = pl.ds(k * SLAB, SLAB)
        copies.append(pltpu.make_async_copy(ens_in.at[at], ens.at[at], sems.at[4 + k]))
    for copy in copies:
        copy.start()
    device = lax.axis_index("gx") * lax.axis_size("gy") + lax.axis_index("gy")
    first = device * (ens.shape[1] // BLK)
    lane = lax.broadcasted_iota(jnp.int32, (SLAB, 128), 1)
    lane8 = lax.broadcasted_iota(jnp.int32, (PAD, 128), 1)
    row8 = lax.broadcasted_iota(jnp.int32, (PAD, 128), 0)
    side = jnp.zeros((PAD, 128), F32)
    for copy in copies[:4]:
        copy.wait()
    for j in range(n):
        b, k = j // slots, j % slots
        block = (first + lax.shift_right_logical(loc[b, k], BLK.bit_length() - 1)).astype(F32)
        live = jnp.where(k < count[0, b], 1.0, 0.0).astype(F32)
        new = jnp.where(
            row8 == 0, block, jnp.where(row8 == 1, values[b, k], jnp.where(row8 == 2, error[b, k], live))
        )
        side = jnp.where(lane8 == j, new, side)
    pieces = []
    for k in range(members // SLAB):
        copies[4 + k].wait()
        acc = jnp.zeros((SLAB, 128), F32)
        for j in range(n):
            c = loc[j // slots, j % slots]
            tile = ens[k * SLAB : (k + 1) * SLAB, pl.ds(pl.multiple_of(c & -128, 128), 128)]
            acc = jnp.where(lane == j, pltpu.roll(tile, (j - c) & 127, 1), acc)
        pieces.append(acc)
    out[...] = jnp.transpose(jnp.concatenate(pieces + [side], axis=0))[:n]


def fetch_kernel(src, dst, sem):
    copy = pltpu.make_async_copy(src, dst, sem.at[0])
    copy.start()
    copy.wait()


def pack_kernel(blocks, weights, list_blocks, list_weights, coef):
    batches, nlist = blocks.shape[:2]
    nb = coef.shape[1]
    lanes = list_blocks.shape[2]
    nx, ny = lax.axis_size("gx"), lax.axis_size("gy")
    ix, iy = lax.axis_index("gx"), lax.axis_index("gy")
    slots = blocks.shape[2] // (nx * ny)
    row_lanes = ny * slots
    first = (ix * ny + iy) * nb
    span = 3 * slots
    lane = lax.broadcasted_iota(jnp.int32, (nlist, 128), 1)
    row = lax.broadcasted_iota(jnp.int32, (nb, 128), 0)
    for b in range(batches):
        w = width(b, batches)
        held_b = [jnp.full((nlist, 128), -1, jnp.int32) for _ in range(lanes // 128)]
        held_w = [jnp.zeros((nlist, 128), F32) for _ in range(lanes // 128)]
        held_c = [jnp.zeros((nb, 128), F32) for _ in range(2)]

        def put(held, tile, d):
            tile = pltpu.roll(tile, (d * span - (iy - 1) * slots + 4 * 128) % 128, 1)
            begin, end = d * span, (d + 1) * span
            for t in range(begin // 128, (end - 1) // 128 + 1):
                keep = (lane >= begin - t * 128) & (lane < end - t * 128)
                held[t] = jnp.where(keep, tile, held[t])

        for d in range(w):
            near = (ix + d - w // 2 + nx) % nx
            at = pl.ds(pl.multiple_of(near * row_lanes, row_lanes), row_lanes)
            bl, wt = blocks[b, :, at], weights[b, :, at]
            put(held_b, bl, d)
            put(held_w, wt, d)
            if abs(d - w // 2) <= 1:
                tile = jnp.zeros((nb, 128), F32)
                for s in range(nb):
                    one = jnp.sum(jnp.where(bl == first + s, wt, 0.0), axis=0, keepdims=True)
                    tile = jnp.where(row == s, one, tile)
                put(held_c, tile, d - w // 2 + 1)
        for t in range(lanes // 128):
            list_blocks[b, :, t * 128 : (t + 1) * 128] = held_b[t]
            list_weights[b, :, t * 128 : (t + 1) * 128] = held_w[t]
        for t in range(2):
            coef[b, :, t * 128 : (t + 1) * 128] = held_c[t]


def along_z_kernel(slots, own, south, north, across, up, down):
    z = lax.axis_index("gx") % ZN
    mine, below, above = own[...], south[...], north[...]
    n = mine.shape[0]
    up[:n] = jnp.where(z == ZN - 1, below, mine)
    up[n:] = jnp.where(z == ZN - 1, mine, above)[: 2 * slots]
    down[:n] = jnp.where(z == 0, above, mine)
    down[n:] = jnp.where(z == 0, mine, below)[: 2 * slots]
    across[: 3 * slots] = jnp.where(z < 2, mine, below)[: 3 * slots]
    across[3 * slots :] = jnp.where(z < 2, above, mine)[: 3 * slots]


def window_kernel(batches, slots, own, south, north, across, up, down, first, rest):
    n = batches * slots
    source = {
        0: (own, 0),
        -4: (south, 0),
        4: (north, 0),
        -1: (up, 0),
        3: (up, n),
        1: (down, 0),
        -3: (down, n),
        -2: (across, 0),
        2: (across, 3 * slots),
    }
    at = 0
    for b in range(batches):
        half = batches - b
        for d in range(-half, half + 1):
            ref, begin = source[d]
            piece = ref[begin + b * slots : begin + (b + 1) * slots]
            if b == 0:
                first[(d + half) * slots : (d + half + 1) * slots] = piece
            else:
                rest[at : at + slots] = piece
                at += slots


def gathered(own, swapped, crossed, slots):
    even = lax.axis_index("gy") % 2 == 0
    a, b, mine = swapped[...], crossed[...], own[...]
    south = jnp.where(even, b, a)
    north = jnp.where(even, a, b)
    pieces = []
    for d in range(mine.shape[0] // slots):
        at = slice(d * slots, (d + 1) * slots)
        pieces += [south[at], mine[at], north[at]]
    return jnp.concatenate(pieces, axis=0)


def mask_of(batch, rest, list_blocks, list_weights, nobs):
    members = rest.shape[1] - PAD
    block = rest[:, members : members + 1].astype(jnp.int32)
    lanes = (nobs + 127) // 128 * 128
    mask = jnp.zeros((rest.shape[0], lanes), F32)
    for l in range(list_blocks.shape[1]):
        mask = mask + jnp.where(
            block == list_blocks[batch, l : l + 1, :lanes], list_weights[batch, l : l + 1, :lanes], 0.0
        )
    return mask


def compose(batch, maps, scaled, increment, coef):
    nb = coef.shape[1]
    members = scaled.shape[1]
    nobs = scaled.shape[0]
    scaled, increment = split(scaled), split(increment)
    s = dot3(split(maps), scaled, NT)
    p = jnp.concatenate(
        [s[k * members : (k + 1) * members] * coef[batch, k : k + 1, :nobs] for k in range(nb)], axis=0
    )
    return maps + dot3(split(p), increment, NN)


def unit(members):
    i = lax.broadcasted_iota(jnp.int32, (members, members), 0)
    j = lax.broadcasted_iota(jnp.int32, (members, members), 1)
    return jnp.where(i == j, 1.0, 0.0).astype(F32)


def mask_kernel(batch, nobs, rest, list_blocks, list_weights, mask):
    mask[...] = mask_of(batch, rest[...], list_blocks, list_weights, nobs)


def map_kernel(batch, scaled, increment, coef, maps, out):
    nb = coef.shape[1]
    start = jnp.concatenate([unit(scaled.shape[1])] * nb, axis=0) if maps is None else maps[...]
    out[...] = compose(batch, start, scaled[...], increment[...], coef)


def step_kernel(slots, own, swapped, crossed, rest, mask, nxt, left, center_s, center_i):
    members = rest.shape[1] - PAD
    scaled, increment = observe(gathered(own, swapped, crossed, slots))
    nobs = scaled.shape[0]
    mid = nobs // (6 * slots) * 3 * slots
    center_s[...] = scaled[mid - 3 * slots : mid + 6 * slots]
    center_i[...] = increment[mid - 3 * slots : mid + 6 * slots]
    rows = rest[...]
    x = rows[:, :members]
    p = dot3(split(x), split(scaled), NT) * mask[:, :nobs]
    x = x + dot3(split(p), split(increment), NN)
    k = nxt.shape[0]
    nxt[:, :members] = x[:k]
    nxt[:, members:] = rows[:k, members:]
    if left is not None:
        left[:, :members] = x[k:]
        left[:, members:] = rows[k:, members:]


def stacked(maps, state):
    mh, ml = split(maps)
    xh, xl = state
    left = jnp.concatenate([mh, ml, mh], axis=0)
    right = jnp.concatenate([xh, xh, xl], axis=0)
    return lax.dot_general(left, right, TN, preferred_element_type=F32)


def early_kernel(maps, ens, state, high, low):
    members = ens.shape[0]
    eye = unit(members)
    for k in range(maps.shape[0] // members):
        at = slice(k * BLK, (k + 1) * BLK)
        x = ens[:, at]
        y = x + stacked(maps[k * members : (k + 1) * members] - eye, split(x))
        state[:, at] = y
        high[:, at], low[:, at] = split(y)


def final_kernel(batch, slots, own, swapped, crossed, coef, state, high, low, out, result, sems):
    nb = coef.shape[1]
    scaled, increment = observe(gathered(own, swapped, crossed, slots))
    nobs, members = scaled.shape
    turned = jnp.transpose(scaled)
    increment = split(increment)
    gains = [dot3(split(turned * coef[batch, k : k + 1, :nobs]), increment, NN) for k in range(nb)]
    copies = []
    for k in range(nb):
        at = slice(k * BLK, (k + 1) * BLK)
        result[:, at] = state[:, at] + stacked(gains[k], (high[:, at], low[:, at]))
        at = pl.ds(k * BLK, BLK)
        copies.append(pltpu.make_async_copy(result.at[:, at], out.at[:, at], sems.at[k]))
        copies[-1].start()
    for copy in copies:
        copy.wait()


def permute(x, target):
    nx, ny = lax.axis_size("gx"), lax.axis_size("gy")
    pairs = []
    for i in range(nx):
        for j in range(ny):
            a, c = target(i, j)
            pairs.append((i * ny + j, (a % nx) * ny + c % ny))
    return lax.ppermute(x, ("gx", "gy"), pairs)


def shards(ensemble, loc, values, error, count, blocks, weights):
    members, rows_here = ensemble.shape
    batches, slots = loc.shape
    nb = rows_here // BLK
    n = batches * slots
    wide = members + PAD
    vm = pl.BlockSpec(memory_space=VMEM)
    hbm = pl.BlockSpec(memory_space=pltpu.HBM)
    tie = pl.BlockSpec(memory_space=pl.ANY)
    params = pltpu.CompilerParams(vmem_limit_bytes=40 * 1024 * 1024)
    shape = lambda *s: jax.ShapeDtypeStruct(s, F32)
    cost = lambda us: pl.CostEstimate(flops=us * 10**6, bytes_accessed=us * 10**5, transcendentals=0)

    own = pl.pallas_call(
        gather_kernel,
        out_shape=shape(n, wide),
        in_specs=[hbm] * 5,
        out_specs=vm,
        scratch_shapes=[
            pltpu.SMEM((batches, slots), jnp.int32),
            pltpu.SMEM((1, batches), jnp.int32),
            pltpu.SMEM((batches, slots), F32),
            pltpu.SMEM((batches, slots), F32),
            pltpu.VMEM((members, rows_here), F32),
            pltpu.SemaphoreType.DMA((4 + members // SLAB,)),
        ],
        compiler_params=pltpu.CompilerParams(vmem_limit_bytes=64 * 1024 * 1024 - 2**21),
        name="gather_columns",
    )(loc, count.reshape(1, batches), values, error, ensemble)

    lanes = (width(0, batches) * 3 * slots + 127) // 128 * 128
    list_blocks, list_weights, coef = pl.pallas_call(
        pack_kernel,
        out_shape=(
            jax.ShapeDtypeStruct((batches, blocks.shape[1], lanes), jnp.int32),
            shape(batches, blocks.shape[1], lanes),
            shape(batches, nb, 256),
        ),
        in_specs=[vm, vm],
        out_specs=(vm, vm, vm),
        compiler_params=params,
        cost_estimate=cost(1),
        name="pack_lists",
    )(blocks, weights)

    south = permute(own, lambda i, j: (i + ZN, j))
    north = permute(own, lambda i, j: (i - ZN, j))
    own = pl.pallas_call(
        fetch_kernel,
        out_shape=shape(n, wide),
        in_specs=[hbm],
        out_specs=vm,
        scratch_shapes=[pltpu.SemaphoreType.DMA((1,))],
        compiler_params=params,
        cost_estimate=cost(1),
        name="fetch_own",
    )(own)
    across, up, down = pl.pallas_call(
        lambda *refs: along_z_kernel(slots, *refs),
        out_shape=(shape(6 * slots, wide), shape(n + 2 * slots, wide), shape(n + 2 * slots, wide)),
        in_specs=[vm] * 3,
        out_specs=(vm,) * 3,
        compiler_params=params,
        name="select_along_z",
    )(own, south, north)
    turn = lambda k: (lambda i, j: (i // ZN * ZN + (i + k) % ZN, j))
    across = permute(across, turn(2))
    up = permute(up, turn(1))
    down = permute(down, turn(ZN - 1))
    total = sum(width(b, batches) for b in range(1, batches)) * slots
    here, rest = pl.pallas_call(
        lambda *refs: window_kernel(batches, slots, *refs),
        out_shape=(shape(width(0, batches) * slots, wide), shape(total, wide)),
        in_specs=[vm] * 6,
        out_specs=(vm, vm),
        compiler_params=params,
        name="lay_out_window",
    )(own, south, north, across, up, down)

    maps = None
    for b in range(batches):
        swapped = permute(here, lambda i, j: (i, j + 1 - 2 * (j % 2)))
        crossed = permute(here, lambda i, j: (i, j + 1 if j % 2 else j - 1))
        if b > 0:
            given = () if maps is None else (maps,)
            body = lambda s, i, c, *r, b=b: map_kernel(b - 1, s, i, c, r[0] if len(r) == 2 else None, r[-1])
            maps = pl.pallas_call(
                body,
                out_shape=shape(nb * members, members),
                in_specs=[vm] * (3 + len(given)),
                out_specs=vm,
                compiler_params=params,
                cost_estimate=cost(1),
                name="compose_maps",
            )(center_s, center_i, coef, *given)
        if b == batches - 1:
            break
        w = width(b, batches)
        nobs = w * 3 * slots
        mask = pl.pallas_call(
            lambda *refs, b=b, nobs=nobs: mask_kernel(b, nobs, *refs),
            out_shape=shape(rest.shape[0], (nobs + 127) // 128 * 128),
            in_specs=[vm] * 3,
            out_specs=vm,
            compiler_params=params,
            cost_estimate=cost(1),
            name="list_mask",
        )(rest, list_blocks, list_weights)
        k = width(b + 1, batches) * slots
        outs = [shape(k, wide), shape(9 * slots, members), shape(9 * slots, members)]
        last = rest.shape[0] == k
        if not last:
            outs.insert(1, shape(rest.shape[0] - k, wide))
            body = lambda *refs: step_kernel(slots, *refs[:5], *refs[-4:])
        else:
            body = lambda *refs: step_kernel(slots, *refs[:5], refs[-3], None, *refs[-2:])
        after = () if maps is None else (maps,)
        res = pl.pallas_call(
            body,
            out_shape=tuple(outs),
            in_specs=[vm] * 5 + [tie] * len(after),
            out_specs=(vm,) * len(outs),
            compiler_params=params,
            name="step_columns",
        )(here, swapped, crossed, rest, mask, *after)
        here, center_s, center_i = res[0], res[-2], res[-1]
        rest = None if last else res[1]

    half = jax.ShapeDtypeStruct((members, rows_here), BF16)
    state = pl.pallas_call(
        early_kernel,
        out_shape=(shape(members, rows_here), half, half),
        in_specs=[vm] * 2,
        out_specs=(vm,) * 3,
        compiler_params=params,
        cost_estimate=cost(1),
        name="apply_early_maps",
    )(maps, ensemble)
    return pl.pallas_call(
        lambda *refs: final_kernel(batches - 1, slots, *refs),
        out_shape=shape(members, rows_here),
        in_specs=[vm] * 7,
        out_specs=hbm,
        scratch_shapes=[pltpu.VMEM((members, rows_here), F32), pltpu.SemaphoreType.DMA((nb,))],
        compiler_params=params,
        name="apply_maps",
    )(here, swapped, crossed, coef, *state)


def solution(mesh):
    split_specs = P(None, ("gx", "gy"))
    in_specs = (split_specs,) * 5 + (P(), P())
    return jax.shard_map(
        shards, mesh=mesh, in_specs=in_specs, out_specs=split_specs, check_vma=False
    )
```

```python
import jax
import jax.numpy as jnp
from jax import lax
from jax.experimental import pallas as pl
from jax.experimental.pallas import tpu as pltpu
from jax.sharding import PartitionSpec as P

BLK = 1024
EPS = 1e-05
ZN = 4
SLAB = 16
PAD = 8
F32 = jnp.float32
BF16 = jnp.bfloat16
VMEM = pltpu.VMEM
NT = (((1,), (1,)), ((), ()))
NN = (((1,), (0,)), ((), ()))
TN = (((0,), (0,)), ((), ()))


def split(x):
    high = x.astype(BF16)
    return high, (x - high.astype(F32)).astype(BF16)


def dot3(a, b, dims):
    ah, al = a
    bh, bl = b
    d = lambda p, q: lax.dot_general(p, q, dims, preferred_element_type=F32)
    return d(ah, bh) + (d(ah, bl) + d(al, bh))


def observe(rows):
    members = rows.shape[1] - PAD
    x = rows[:, :members]
    value, error, live = (rows[:, members + k : members + k + 1] for k in (1, 2, 3))
    mean = jnp.sum(x, axis=1, keepdims=True) / members
    anomaly = x - mean
    var = jnp.sum(anomaly * anomaly, axis=1, keepdims=True) / (members - 1) + EPS
    increment = (
        var / (var + error) * (value - mean) + (jnp.sqrt(error / (var + error)) - 1.0) * anomaly
    )
    centred = anomaly - jnp.sum(anomaly, axis=1, keepdims=True) / members
    return centred * (live / ((members - 1) * var)), increment


def width(batch, batches):
    return 2 * (batches - batch) + 1


def gather_kernel(loc_in, count_in, value_in, error_in, ens_in, out, loc, count, values, error, ens, sems):
    members = ens.shape[0]
    batches, slots = loc.shape
    n = batches * slots
    small = [(loc_in, loc), (count_in, count), (value_in, values), (error_in, error)]
    copies = [pltpu.make_async_copy(src, dst, sems.at[k]) for k, (src, dst) in enumerate(small)]
    for k in range(members // SLAB):
        at = pl.ds(k * SLAB, SLAB)
        copies.append(pltpu.make_async_copy(ens_in.at[at], ens.at[at], sems.at[4 + k]))
    for copy in copies:
        copy.start()
    device = lax.axis_index("gx") * lax.axis_size("gy") + lax.axis_index("gy")
    first = device * (ens.shape[1] // BLK)
    lane = lax.broadcasted_iota(jnp.int32, (SLAB, 128), 1)
    lane8 = lax.broadcasted_iota(jnp.int32, (PAD, 128), 1)
    row8 = lax.broadcasted_iota(jnp.int32, (PAD, 128), 0)
    side = jnp.zeros((PAD, 128), F32)
    for copy in copies[:4]:
        copy.wait()
    for j in range(n):
        b, k = j // slots, j % slots
        block = (first + lax.shift_right_logical(loc[b, k], BLK.bit_length() - 1)).astype(F32)
        live = jnp.where(k < count[0, b], 1.0, 0.0).astype(F32)
        new = jnp.where(
            row8 == 0, block, jnp.where(row8 == 1, values[b, k], jnp.where(row8 == 2, error[b, k], live))
        )
        side = jnp.where(lane8 == j, new, side)
    pieces = []
    for k in range(members // SLAB):
        copies[4 + k].wait()
        acc = jnp.zeros((SLAB, 128), F32)
        for j in range(n):
            c = loc[j // slots, j % slots]
            tile = ens[k * SLAB : (k + 1) * SLAB, pl.ds(pl.multiple_of(c & -128, 128), 128)]
            acc = jnp.where(lane == j, pltpu.roll(tile, (j - c) & 127, 1), acc)
        pieces.append(acc)
    out[...] = jnp.transpose(jnp.concatenate(pieces + [side], axis=0))[:n]


def fetch_kernel(src, dst, sem):
    copy = pltpu.make_async_copy(src, dst, sem.at[0])
    copy.start()
    copy.wait()


def pack_kernel(blocks, weights, list_blocks, list_weights, coef):
    batches, nlist = blocks.shape[:2]
    nb = coef.shape[1]
    lanes = list_blocks.shape[2]
    nx, ny = lax.axis_size("gx"), lax.axis_size("gy")
    ix, iy = lax.axis_index("gx"), lax.axis_index("gy")
    slots = blocks.shape[2] // (nx * ny)
    row_lanes = ny * slots
    first = (ix * ny + iy) * nb
    span = 3 * slots
    lane = lax.broadcasted_iota(jnp.int32, (nlist, 128), 1)
    row = lax.broadcasted_iota(jnp.int32, (nb, 128), 0)
    for b in range(batches):
        w = width(b, batches)
        held_b = [jnp.full((nlist, 128), -1, jnp.int32) for _ in range(lanes // 128)]
        held_w = [jnp.zeros((nlist, 128), F32) for _ in range(lanes // 128)]
        held_c = [jnp.zeros((nb, 128), F32) for _ in range(2)]

        def put(held, tile, d):
            tile = pltpu.roll(tile, (d * span - (iy - 1) * slots + 4 * 128) % 128, 1)
            begin, end = d * span, (d + 1) * span
            for t in range(begin // 128, (end - 1) // 128 + 1):
                keep = (lane >= begin - t * 128) & (lane < end - t * 128)
                held[t] = jnp.where(keep, tile, held[t])

        for d in range(w):
            near = (ix + d - w // 2 + nx) % nx
            at = pl.ds(pl.multiple_of(near * row_lanes, row_lanes), row_lanes)
            bl, wt = blocks[b, :, at], weights[b, :, at]
            put(held_b, bl, d)
            put(held_w, wt, d)
            if abs(d - w // 2) <= 1:
                tile = jnp.zeros((nb, 128), F32)
                for s in range(nb):
                    one = jnp.sum(jnp.where(bl == first + s, wt, 0.0), axis=0, keepdims=True)
                    tile = jnp.where(row == s, one, tile)
                put(held_c, tile, d - w // 2 + 1)
        for t in range(lanes // 128):
            list_blocks[b, :, t * 128 : (t + 1) * 128] = held_b[t]
            list_weights[b, :, t * 128 : (t + 1) * 128] = held_w[t]
        for t in range(2):
            coef[b, :, t * 128 : (t + 1) * 128] = held_c[t]


def by_parity(odd, a, b):
    return jnp.where(odd, b, a), jnp.where(odd, a, b)


def along_z_kernel(slots, own, inner, outer, across, away, beside):
    gx = lax.axis_index("gx")
    z, odd_y = gx % ZN, gx // ZN % 2 == 1
    mine = own[...]
    above, below = by_parity(odd_y, inner[...], outer[...])
    up = jnp.concatenate(
        [jnp.where(z == ZN - 1, below, mine), jnp.where(z == ZN - 1, mine, above)[: 2 * slots]], axis=0
    )
    down = jnp.concatenate(
        [jnp.where(z == 0, above, mine), jnp.where(z == 0, mine, below)[: 2 * slots]], axis=0
    )
    across[: 3 * slots] = jnp.where(z < 2, mine, below)[: 3 * slots]
    across[3 * slots :] = jnp.where(z < 2, above, mine)[: 3 * slots]
    beside[...], away[...] = by_parity(z % 2 == 1, up, down)


def window_kernel(batches, slots, own, inner, outer, across, away, beside, first, rest):
    n = batches * slots
    gx = lax.axis_index("gx")
    north, south = by_parity(gx // ZN % 2 == 1, inner[:slots], outer[:slots])
    down, up = by_parity(gx % 2 == 1, beside[...], away[...])
    source = {
        0: (own, 0),
        -4: (south, 0),
        4: (north, 0),
        -1: (up, 0),
        3: (up, n),
        1: (down, 0),
        -3: (down, n),
        -2: (across, 0),
        2: (across, 3 * slots),
    }
    at = 0
    for b in range(batches):
        half = batches - b
        for d in range(-half, half + 1):
            ref, begin = source[d]
            piece = ref[begin + b * slots : begin + (b + 1) * slots]
            if b == 0:
                first[(d + half) * slots : (d + half + 1) * slots] = piece
            else:
                rest[at : at + slots] = piece
                at += slots


def gathered(own, swapped, crossed, slots):
    even = lax.axis_index("gy") % 2 == 0
    a, b, mine = swapped[...], crossed[...], own[...]
    south = jnp.where(even, b, a)
    north = jnp.where(even, a, b)
    pieces = []
    for d in range(mine.shape[0] // slots):
        at = slice(d * slots, (d + 1) * slots)
        pieces += [south[at], mine[at], north[at]]
    return jnp.concatenate(pieces, axis=0)


def mask_of(batch, rest, list_blocks, list_weights, nobs):
    members = rest.shape[1] - PAD
    block = rest[:, members : members + 1].astype(jnp.int32)
    lanes = (nobs + 127) // 128 * 128
    mask = jnp.zeros((rest.shape[0], lanes), F32)
    for l in range(list_blocks.shape[1]):
        mask = mask + jnp.where(
            block == list_blocks[batch, l : l + 1, :lanes], list_weights[batch, l : l + 1, :lanes], 0.0
        )
    return mask


def compose(batch, maps, scaled, increment, coef):
    nb = coef.shape[1]
    members = scaled.shape[1]
    nobs = scaled.shape[0]
    scaled, increment = split(scaled), split(increment)
    s = dot3(split(maps), scaled, NT)
    p = jnp.concatenate(
        [s[k * members : (k + 1) * members] * coef[batch, k : k + 1, :nobs] for k in range(nb)], axis=0
    )
    return maps + dot3(split(p), increment, NN)


def unit(members):
    i = lax.broadcasted_iota(jnp.int32, (members, members), 0)
    j = lax.broadcasted_iota(jnp.int32, (members, members), 1)
    return jnp.where(i == j, 1.0, 0.0).astype(F32)


def mask_kernel(batch, nobs, rest, list_blocks, list_weights, mask):
    mask[...] = mask_of(batch, rest[...], list_blocks, list_weights, nobs)


def map_kernel(batch, scaled, increment, coef, maps, out):
    nb = coef.shape[1]
    start = jnp.concatenate([unit(scaled.shape[1])] * nb, axis=0) if maps is None else maps[...]
    out[...] = compose(batch, start, scaled[...], increment[...], coef)


def step_kernel(slots, own, swapped, crossed, rest, mask, nxt, left, center_s, center_i):
    members = rest.shape[1] - PAD
    scaled, increment = observe(gathered(own, swapped, crossed, slots))
    nobs = scaled.shape[0]
    mid = nobs // (6 * slots) * 3 * slots
    center_s[...] = scaled[mid - 3 * slots : mid + 6 * slots]
    center_i[...] = increment[mid - 3 * slots : mid + 6 * slots]
    rows = rest[...]
    x = rows[:, :members]
    p = dot3(split(x), split(scaled), NT) * mask[:, :nobs]
    x = x + dot3(split(p), split(increment), NN)
    k = nxt.shape[0]
    nxt[:, :members] = x[:k]
    nxt[:, members:] = rows[:k, members:]
    if left is not None:
        left[:, :members] = x[k:]
        left[:, members:] = rows[k:, members:]


def stacked(maps, state):
    mh, ml = split(maps)
    xh, xl = state
    left = jnp.concatenate([mh, ml, mh], axis=0)
    right = jnp.concatenate([xh, xh, xl], axis=0)
    return lax.dot_general(left, right, TN, preferred_element_type=F32)


def early_kernel(maps, ens, state, high, low):
    members = ens.shape[0]
    eye = unit(members)
    for k in range(maps.shape[0] // members):
        at = slice(k * BLK, (k + 1) * BLK)
        x = ens[:, at]
        y = x + stacked(maps[k * members : (k + 1) * members] - eye, split(x))
        state[:, at] = y
        high[:, at], low[:, at] = split(y)


def final_kernel(batch, slots, own, swapped, crossed, coef, state, high, low, out, result, sems):
    nb = coef.shape[1]
    scaled, increment = observe(gathered(own, swapped, crossed, slots))
    nobs, members = scaled.shape
    turned = jnp.transpose(scaled)
    increment = split(increment)
    gains = [dot3(split(turned * coef[batch, k : k + 1, :nobs]), increment, NN) for k in range(nb)]
    copies = []
    for k in range(nb):
        at = slice(k * BLK, (k + 1) * BLK)
        result[:, at] = state[:, at] + stacked(gains[k], (high[:, at], low[:, at]))
        at = pl.ds(k * BLK, BLK)
        copies.append(pltpu.make_async_copy(result.at[:, at], out.at[:, at], sems.at[k]))
        copies[-1].start()
    for copy in copies:
        copy.wait()


def permute(x, target):
    nx, ny = lax.axis_size("gx"), lax.axis_size("gy")
    pairs = []
    for i in range(nx):
        for j in range(ny):
            a, c = target(i, j)
            pairs.append((i * ny + j, (a % nx) * ny + c % ny))
    return lax.ppermute(x, ("gx", "gy"), pairs)


def shards(ensemble, loc, values, error, count, blocks, weights):
    members, rows_here = ensemble.shape
    batches, slots = loc.shape
    nb = rows_here // BLK
    n = batches * slots
    wide = members + PAD
    vm = pl.BlockSpec(memory_space=VMEM)
    hbm = pl.BlockSpec(memory_space=pltpu.HBM)
    tie = pl.BlockSpec(memory_space=pl.ANY)
    params = pltpu.CompilerParams(vmem_limit_bytes=40 * 1024 * 1024)
    shape = lambda *s: jax.ShapeDtypeStruct(s, F32)
    cost = lambda us: pl.CostEstimate(flops=us * 10**6, bytes_accessed=us * 10**5, transcendentals=0)

    own = pl.pallas_call(
        gather_kernel,
        out_shape=shape(n, wide),
        in_specs=[hbm] * 5,
        out_specs=vm,
        scratch_shapes=[
            pltpu.SMEM((batches, slots), jnp.int32),
            pltpu.SMEM((1, batches), jnp.int32),
            pltpu.SMEM((batches, slots), F32),
            pltpu.SMEM((batches, slots), F32),
            pltpu.VMEM((members, rows_here), F32),
            pltpu.SemaphoreType.DMA((4 + members // SLAB,)),
        ],
        compiler_params=pltpu.CompilerParams(vmem_limit_bytes=64 * 1024 * 1024 - 2**21),
        name="gather_columns",
    )(loc, count.reshape(1, batches), values, error, ensemble)

    lanes = (width(0, batches) * 3 * slots + 127) // 128 * 128
    list_blocks, list_weights, coef = pl.pallas_call(
        pack_kernel,
        out_shape=(
            jax.ShapeDtypeStruct((batches, blocks.shape[1], lanes), jnp.int32),
            shape(batches, blocks.shape[1], lanes),
            shape(batches, nb, 256),
        ),
        in_specs=[vm, vm],
        out_specs=(vm, vm, vm),
        compiler_params=params,
        cost_estimate=cost(1),
        name="pack_lists",
    )(blocks, weights)

    pair_y = lambda odd: (lambda i, j: (i + ZN if (i // ZN + odd) % 2 == 0 else i - ZN, j))
    pair_z = lambda odd: (
        lambda i, j: (i // ZN * ZN + (i + (1 if (i + odd) % 2 == 0 else ZN - 1)) % ZN, j)
    )
    outer = permute(own, pair_y(1))
    inner = permute(own, pair_y(0))
    own = pl.pallas_call(
        fetch_kernel,
        out_shape=shape(n, wide),
        in_specs=[hbm],
        out_specs=vm,
        scratch_shapes=[pltpu.SemaphoreType.DMA((1,))],
        compiler_params=params,
        cost_estimate=cost(1),
        name="fetch_own",
    )(own)
    across, away, beside = pl.pallas_call(
        lambda *refs: along_z_kernel(slots, *refs),
        out_shape=(shape(6 * slots, wide), shape(n + 2 * slots, wide), shape(n + 2 * slots, wide)),
        in_specs=[vm] * 3,
        out_specs=(vm,) * 3,
        compiler_params=params,
        name="select_along_z",
    )(own, inner, outer)
    across = permute(across, lambda i, j: (i // ZN * ZN + (i + 2) % ZN, j))
    away = permute(away, pair_z(1))
    beside = permute(beside, pair_z(0))
    total = sum(width(b, batches) for b in range(1, batches)) * slots
    here, rest = pl.pallas_call(
        lambda *refs: window_kernel(batches, slots, *refs),
        out_shape=(shape(width(0, batches) * slots, wide), shape(total, wide)),
        in_specs=[vm] * 6,
        out_specs=(vm, vm),
        compiler_params=params,
        name="lay_out_window",
    )(own, inner, outer, across, away, beside)

    maps = None
    for b in range(batches):
        swapped = permute(here, lambda i, j: (i, j + 1 - 2 * (j % 2)))
        crossed = permute(here, lambda i, j: (i, j + 1 if j % 2 else j - 1))
        if b > 0:
            given = () if maps is None else (maps,)
            body = lambda s, i, c, *r, b=b: map_kernel(b - 1, s, i, c, r[0] if len(r) == 2 else None, r[-1])
            maps = pl.pallas_call(
                body,
                out_shape=shape(nb * members, members),
                in_specs=[vm] * (3 + len(given)),
                out_specs=vm,
                compiler_params=params,
                cost_estimate=cost(1),
                name="compose_maps",
            )(center_s, center_i, coef, *given)
        if b == batches - 1:
            break
        w = width(b, batches)
        nobs = w * 3 * slots
        mask = pl.pallas_call(
            lambda *refs, b=b, nobs=nobs: mask_kernel(b, nobs, *refs),
            out_shape=shape(rest.shape[0], (nobs + 127) // 128 * 128),
            in_specs=[vm] * 3,
            out_specs=vm,
            compiler_params=params,
            cost_estimate=cost(1),
            name="list_mask",
        )(rest, list_blocks, list_weights)
        k = width(b + 1, batches) * slots
        outs = [shape(k, wide), shape(9 * slots, members), shape(9 * slots, members)]
        last = rest.shape[0] == k
        if not last:
            outs.insert(1, shape(rest.shape[0] - k, wide))
            body = lambda *refs: step_kernel(slots, *refs[:5], *refs[-4:])
        else:
            body = lambda *refs: step_kernel(slots, *refs[:5], refs[-3], None, *refs[-2:])
        after = () if maps is None else (maps,)
        res = pl.pallas_call(
            body,
            out_shape=tuple(outs),
            in_specs=[vm] * 5 + [tie] * len(after),
            out_specs=(vm,) * len(outs),
            compiler_params=params,
            name="step_columns",
        )(here, swapped, crossed, rest, mask, *after)
        here, center_s, center_i = res[0], res[-2], res[-1]
        rest = None if last else res[1]

    half = jax.ShapeDtypeStruct((members, rows_here), BF16)
    state = pl.pallas_call(
        early_kernel,
        out_shape=(shape(members, rows_here), half, half),
        in_specs=[vm] * 2,
        out_specs=(vm,) * 3,
        compiler_params=params,
        cost_estimate=cost(1),
        name="apply_early_maps",
    )(maps, ensemble)
    return pl.pallas_call(
        lambda *refs: final_kernel(batches - 1, slots, *refs),
        out_shape=shape(members, rows_here),
        in_specs=[vm] * 7,
        out_specs=hbm,
        scratch_shapes=[pltpu.VMEM((members, rows_here), F32), pltpu.SemaphoreType.DMA((nb,))],
        compiler_params=params,
        name="apply_maps",
    )(here, swapped, crossed, coef, *state)


def solution(mesh):
    split_specs = P(None, ("gx", "gy"))
    in_specs = (split_specs,) * 5 + (P(), P())
    return jax.shard_map(
        shards, mesh=mesh, in_specs=in_specs, out_specs=split_specs, check_vma=False
    )
```

```python
import jax
import jax.numpy as jnp
from jax import lax
from jax.experimental import pallas as pl
from jax.experimental.pallas import tpu as pltpu
from jax.sharding import PartitionSpec as P

BLK = 1024
EPS = 1e-05
ZN = 4
SLAB = 16
PAD = 8
F32 = jnp.float32
BF16 = jnp.bfloat16
VMEM = pltpu.VMEM
NT = (((1,), (1,)), ((), ()))
NN = (((1,), (0,)), ((), ()))
TN = (((0,), (0,)), ((), ()))


def split(x):
    high = x.astype(BF16)
    return high, (x - high.astype(F32)).astype(BF16)


def dot3(a, b, dims):
    ah, al = a
    bh, bl = b
    d = lambda p, q: lax.dot_general(p, q, dims, preferred_element_type=F32)
    return d(ah, bh) + (d(ah, bl) + d(al, bh))


def observe(rows):
    members = rows.shape[1] - PAD
    x = rows[:, :members]
    value, error, live = (rows[:, members + k : members + k + 1] for k in (1, 2, 3))
    mean = jnp.sum(x, axis=1, keepdims=True) / members
    anomaly = x - mean
    var = jnp.sum(anomaly * anomaly, axis=1, keepdims=True) / (members - 1) + EPS
    increment = (
        var / (var + error) * (value - mean) + (jnp.sqrt(error / (var + error)) - 1.0) * anomaly
    )
    centred = anomaly - jnp.sum(anomaly, axis=1, keepdims=True) / members
    return centred * (live / ((members - 1) * var)), increment


def width(batch, batches):
    return 2 * (batches - batch) + 1


def gather_kernel(loc_in, count_in, value_in, error_in, ens_in, out, loc, count, values, error, ens, sems):
    members = ens.shape[0]
    batches, slots = loc.shape
    n = batches * slots
    small = [(loc_in, loc), (count_in, count), (value_in, values), (error_in, error)]
    copies = [pltpu.make_async_copy(src, dst, sems.at[k]) for k, (src, dst) in enumerate(small)]
    for k in range(members // SLAB):
        at = pl.ds(k * SLAB, SLAB)
        copies.append(pltpu.make_async_copy(ens_in.at[at], ens.at[at], sems.at[4 + k]))
    for copy in copies:
        copy.start()
    device = lax.axis_index("gx") * lax.axis_size("gy") + lax.axis_index("gy")
    first = device * (ens.shape[1] // BLK)
    lane = lax.broadcasted_iota(jnp.int32, (SLAB, 128), 1)
    lane8 = lax.broadcasted_iota(jnp.int32, (PAD, 128), 1)
    row8 = lax.broadcasted_iota(jnp.int32, (PAD, 128), 0)
    side = jnp.zeros((PAD, 128), F32)
    for copy in copies[:4]:
        copy.wait()
    for j in range(n):
        b, k = j // slots, j % slots
        block = (first + lax.shift_right_logical(loc[b, k], BLK.bit_length() - 1)).astype(F32)
        live = jnp.where(k < count[0, b], 1.0, 0.0).astype(F32)
        new = jnp.where(
            row8 == 0, block, jnp.where(row8 == 1, values[b, k], jnp.where(row8 == 2, error[b, k], live))
        )
        side = jnp.where(lane8 == j, new, side)
    pieces = []
    for k in range(members // SLAB):
        copies[4 + k].wait()
        acc = jnp.zeros((SLAB, 128), F32)
        for j in range(n):
            c = loc[j // slots, j % slots]
            tile = ens[k * SLAB : (k + 1) * SLAB, pl.ds(pl.multiple_of(c & -128, 128), 128)]
            acc = jnp.where(lane == j, pltpu.roll(tile, (j - c) & 127, 1), acc)
        pieces.append(acc)
    out[...] = jnp.transpose(jnp.concatenate(pieces + [side], axis=0))[:n]


def fetch_kernel(src, dst, sem):
    copy = pltpu.make_async_copy(src, dst, sem.at[0])
    copy.start()
    copy.wait()


def pack_kernel(blocks, weights, list_blocks, list_weights, coef):
    batches, nlist = blocks.shape[:2]
    nb = coef.shape[1]
    lanes = list_blocks.shape[2]
    nx, ny = lax.axis_size("gx"), lax.axis_size("gy")
    ix, iy = lax.axis_index("gx"), lax.axis_index("gy")
    slots = blocks.shape[2] // (nx * ny)
    row_lanes = ny * slots
    first = (ix * ny + iy) * nb
    span = 3 * slots
    lane = lax.broadcasted_iota(jnp.int32, (nlist, 128), 1)
    row = lax.broadcasted_iota(jnp.int32, (nb, 128), 0)
    for b in range(batches):
        w = width(b, batches)
        held_b = [jnp.full((nlist, 128), -1, jnp.int32) for _ in range(lanes // 128)]
        held_w = [jnp.zeros((nlist, 128), F32) for _ in range(lanes // 128)]
        held_c = [jnp.zeros((nb, 128), F32) for _ in range(2)]

        def put(held, tile, d):
            tile = pltpu.roll(tile, (d * span - (iy - 1) * slots + 4 * 128) % 128, 1)
            begin, end = d * span, (d + 1) * span
            for t in range(begin // 128, (end - 1) // 128 + 1):
                keep = (lane >= begin - t * 128) & (lane < end - t * 128)
                held[t] = jnp.where(keep, tile, held[t])

        for d in range(w):
            near = (ix + d - w // 2 + nx) % nx
            at = pl.ds(pl.multiple_of(near * row_lanes, row_lanes), row_lanes)
            bl, wt = blocks[b, :, at], weights[b, :, at]
            put(held_b, bl, d)
            put(held_w, wt, d)
            if abs(d - w // 2) <= 1:
                tile = jnp.zeros((nb, 128), F32)
                for s in range(nb):
                    one = jnp.sum(jnp.where(bl == first + s, wt, 0.0), axis=0, keepdims=True)
                    tile = jnp.where(row == s, one, tile)
                put(held_c, tile, d - w // 2 + 1)
        for t in range(lanes // 128):
            list_blocks[b, :, t * 128 : (t + 1) * 128] = held_b[t]
            list_weights[b, :, t * 128 : (t + 1) * 128] = held_w[t]
        for t in range(2):
            coef[b, :, t * 128 : (t + 1) * 128] = held_c[t]


def by_parity(odd, a, b):
    return jnp.where(odd, b, a), jnp.where(odd, a, b)


def along_z_kernel(slots, own, inner, outer, across, away, beside):
    gx = lax.axis_index("gx")
    z, odd_y = gx % ZN, gx // ZN % 2 == 1
    mine = own[...]
    above, below = by_parity(odd_y, inner[...], outer[...])
    up = jnp.concatenate(
        [jnp.where(z == ZN - 1, below, mine), jnp.where(z == ZN - 1, mine, above)[: 2 * slots]], axis=0
    )
    down = jnp.concatenate(
        [jnp.where(z == 0, above, mine), jnp.where(z == 0, mine, below)[: 2 * slots]], axis=0
    )
    across[: 3 * slots] = jnp.where(z < 2, mine, below)[: 3 * slots]
    across[3 * slots :] = jnp.where(z < 2, above, mine)[: 3 * slots]
    beside[...], away[...] = by_parity(z % 2 == 1, up, down)


def window_kernel(batches, slots, own, inner, outer, across, away, beside, first, rest):
    n = batches * slots
    gx = lax.axis_index("gx")
    north, south = by_parity(gx // ZN % 2 == 1, inner[:slots], outer[:slots])
    down, up = by_parity(gx % 2 == 1, beside[...], away[...])
    source = {
        0: (own, 0),
        -4: (south, 0),
        4: (north, 0),
        -1: (up, 0),
        3: (up, n),
        1: (down, 0),
        -3: (down, n),
        -2: (across, 0),
        2: (across, 3 * slots),
    }
    at = 0
    for b in range(batches):
        half = batches - b
        for d in range(-half, half + 1):
            ref, begin = source[d]
            piece = ref[begin + b * slots : begin + (b + 1) * slots]
            if b == 0:
                first[(d + half) * slots : (d + half + 1) * slots] = piece
            else:
                rest[at : at + slots] = piece
                at += slots


def gathered(own, swapped, crossed, slots):
    even = lax.axis_index("gy") % 2 == 0
    a, b, mine = swapped[...], crossed[...], own[...]
    south = jnp.where(even, b, a)
    north = jnp.where(even, a, b)
    pieces = []
    for d in range(mine.shape[0] // slots):
        at = slice(d * slots, (d + 1) * slots)
        pieces += [south[at], mine[at], north[at]]
    return jnp.concatenate(pieces, axis=0)


def mask_of(batch, rest, list_blocks, list_weights, nobs):
    members = rest.shape[1] - PAD
    block = rest[:, members : members + 1].astype(jnp.int32)
    lanes = (nobs + 127) // 128 * 128
    mask = jnp.zeros((rest.shape[0], lanes), F32)
    for l in range(list_blocks.shape[1]):
        mask = mask + jnp.where(
            block == list_blocks[batch, l : l + 1, :lanes], list_weights[batch, l : l + 1, :lanes], 0.0
        )
    return mask


def compose(batch, maps, scaled, increment, coef):
    nb = coef.shape[1]
    members = scaled.shape[1]
    nobs = scaled.shape[0]
    scaled, increment = split(scaled), split(increment)
    s = dot3(split(maps), scaled, NT)
    p = jnp.concatenate(
        [s[k * members : (k + 1) * members] * coef[batch, k : k + 1, :nobs] for k in range(nb)], axis=0
    )
    return maps + dot3(split(p), increment, NN)


def unit(members):
    i = lax.broadcasted_iota(jnp.int32, (members, members), 0)
    j = lax.broadcasted_iota(jnp.int32, (members, members), 1)
    return jnp.where(i == j, 1.0, 0.0).astype(F32)


def mask_kernel(batch, nobs, rest, list_blocks, list_weights, mask):
    mask[...] = mask_of(batch, rest[...], list_blocks, list_weights, nobs)


def map_kernel(batch, scaled, increment, coef, maps, out):
    nb = coef.shape[1]
    start = jnp.concatenate([unit(scaled.shape[1])] * nb, axis=0) if maps is None else maps[...]
    out[...] = compose(batch, start, scaled[...], increment[...], coef)


def step_kernel(slots, begin, end, own, swapped, crossed, rest, mask, out, center_s=None, center_i=None):
    members = rest.shape[1] - PAD
    scaled, increment = observe(gathered(own, swapped, crossed, slots))
    nobs = scaled.shape[0]
    if center_s is not None:
        mid = nobs // (6 * slots) * 3 * slots
        center_s[...] = scaled[mid - 3 * slots : mid + 6 * slots]
        center_i[...] = increment[mid - 3 * slots : mid + 6 * slots]
    x = rest[begin:end, :members]
    p = dot3(split(x), split(scaled), NT) * mask[begin:end, :nobs]
    out[:, :members] = x + dot3(split(p), split(increment), NN)
    out[:, members:] = rest[begin:end, members:]


def stacked(maps, state):
    mh, ml = split(maps)
    xh, xl = state
    left = jnp.concatenate([mh, ml, mh], axis=0)
    right = jnp.concatenate([xh, xh, xl], axis=0)
    return lax.dot_general(left, right, TN, preferred_element_type=F32)


def early_kernel(maps, ens, state, high, low):
    members = ens.shape[0]
    eye = unit(members)
    for k in range(maps.shape[0] // members):
        at = slice(k * BLK, (k + 1) * BLK)
        x = ens[:, at]
        y = x + stacked(maps[k * members : (k + 1) * members] - eye, split(x))
        state[:, at] = y
        high[:, at], low[:, at] = split(y)


def final_kernel(batch, slots, own, swapped, crossed, coef, state, high, low, out, result, sems):
    nb = coef.shape[1]
    scaled, increment = observe(gathered(own, swapped, crossed, slots))
    nobs, members = scaled.shape
    turned = jnp.transpose(scaled)
    increment = split(increment)
    gains = [dot3(split(turned * coef[batch, k : k + 1, :nobs]), increment, NN) for k in range(nb)]
    copies = []
    for k in range(nb):
        at = slice(k * BLK, (k + 1) * BLK)
        result[:, at] = state[:, at] + stacked(gains[k], (high[:, at], low[:, at]))
        at = pl.ds(k * BLK, BLK)
        copies.append(pltpu.make_async_copy(result.at[:, at], out.at[:, at], sems.at[k]))
        copies[-1].start()
    for copy in copies:
        copy.wait()


def permute(x, target):
    nx, ny = lax.axis_size("gx"), lax.axis_size("gy")
    pairs = []
    for i in range(nx):
        for j in range(ny):
            a, c = target(i, j)
            pairs.append((i * ny + j, (a % nx) * ny + c % ny))
    return lax.ppermute(x, ("gx", "gy"), pairs)


def shards(ensemble, loc, values, error, count, blocks, weights):
    members, rows_here = ensemble.shape
    batches, slots = loc.shape
    nb = rows_here // BLK
    n = batches * slots
    wide = members + PAD
    vm = pl.BlockSpec(memory_space=VMEM)
    hbm = pl.BlockSpec(memory_space=pltpu.HBM)
    tie = pl.BlockSpec(memory_space=pl.ANY)
    params = pltpu.CompilerParams(vmem_limit_bytes=40 * 1024 * 1024)
    shape = lambda *s: jax.ShapeDtypeStruct(s, F32)
    cost = lambda us: pl.CostEstimate(flops=us * 10**6, bytes_accessed=us * 10**5, transcendentals=0)

    own = pl.pallas_call(
        gather_kernel,
        out_shape=shape(n, wide),
        in_specs=[hbm] * 5,
        out_specs=vm,
        scratch_shapes=[
            pltpu.SMEM((batches, slots), jnp.int32),
            pltpu.SMEM((1, batches), jnp.int32),
            pltpu.SMEM((batches, slots), F32),
            pltpu.SMEM((batches, slots), F32),
            pltpu.VMEM((members, rows_here), F32),
            pltpu.SemaphoreType.DMA((4 + members // SLAB,)),
        ],
        compiler_params=pltpu.CompilerParams(vmem_limit_bytes=64 * 1024 * 1024 - 2**21),
        name="gather_columns",
    )(loc, count.reshape(1, batches), values, error, ensemble)

    lanes = (width(0, batches) * 3 * slots + 127) // 128 * 128
    list_blocks, list_weights, coef = pl.pallas_call(
        pack_kernel,
        out_shape=(
            jax.ShapeDtypeStruct((batches, blocks.shape[1], lanes), jnp.int32),
            shape(batches, blocks.shape[1], lanes),
            shape(batches, nb, 256),
        ),
        in_specs=[vm, vm],
        out_specs=(vm, vm, vm),
        compiler_params=params,
        cost_estimate=cost(1),
        name="pack_lists",
    )(blocks, weights)

    pair_y = lambda odd: (lambda i, j: (i + ZN if (i // ZN + odd) % 2 == 0 else i - ZN, j))
    pair_z = lambda odd: (
        lambda i, j: (i // ZN * ZN + (i + (1 if (i + odd) % 2 == 0 else ZN - 1)) % ZN, j)
    )
    outer = permute(own, pair_y(1))
    inner = permute(own, pair_y(0))
    own = pl.pallas_call(
        fetch_kernel,
        out_shape=shape(n, wide),
        in_specs=[hbm],
        out_specs=vm,
        scratch_shapes=[pltpu.SemaphoreType.DMA((1,))],
        compiler_params=params,
        cost_estimate=cost(1),
        name="fetch_own",
    )(own)
    across, away, beside = pl.pallas_call(
        lambda *refs: along_z_kernel(slots, *refs),
        out_shape=(shape(6 * slots, wide), shape(n + 2 * slots, wide), shape(n + 2 * slots, wide)),
        in_specs=[vm] * 3,
        out_specs=(vm,) * 3,
        compiler_params=params,
        name="select_along_z",
    )(own, inner, outer)
    across = permute(across, lambda i, j: (i // ZN * ZN + (i + 2) % ZN, j))
    away = permute(away, pair_z(1))
    beside = permute(beside, pair_z(0))
    total = sum(width(b, batches) for b in range(1, batches)) * slots
    here, rest = pl.pallas_call(
        lambda *refs: window_kernel(batches, slots, *refs),
        out_shape=(shape(width(0, batches) * slots, wide), shape(total, wide)),
        in_specs=[vm] * 6,
        out_specs=(vm, vm),
        compiler_params=params,
        name="lay_out_window",
    )(own, inner, outer, across, away, beside)

    maps = None
    for b in range(batches):
        swapped = permute(here, lambda i, j: (i, j + 1 - 2 * (j % 2)))
        crossed = permute(here, lambda i, j: (i, j + 1 if j % 2 else j - 1))
        if b > 0:
            given = () if maps is None else (maps,)
            body = lambda s, i, c, *r, b=b: map_kernel(b - 1, s, i, c, r[0] if len(r) == 2 else None, r[-1])
            maps = pl.pallas_call(
                body,
                out_shape=shape(nb * members, members),
                in_specs=[vm] * (3 + len(given)),
                out_specs=vm,
                compiler_params=params,
                cost_estimate=cost(1),
                name="compose_maps",
            )(center_s, center_i, coef, *given)
        if b == batches - 1:
            break
        w = width(b, batches)
        nobs = w * 3 * slots
        mask = pl.pallas_call(
            lambda *refs, b=b, nobs=nobs: mask_kernel(b, nobs, *refs),
            out_shape=shape(rest.shape[0], (nobs + 127) // 128 * 128),
            in_specs=[vm] * 3,
            out_specs=vm,
            compiler_params=params,
            cost_estimate=cost(1),
            name="list_mask",
        )(rest, list_blocks, list_weights)
        k = width(b + 1, batches) * slots
        given = (here, swapped, crossed, rest, mask)
        centers = (shape(9 * slots, members),) * 2

        def step(begin, end, more, after):
            return pl.pallas_call(
                lambda *refs: step_kernel(slots, begin, end, *refs[:5], *refs[5 + len(after) :]),
                out_shape=(shape(end - begin, wide),) + more,
                in_specs=[vm] * 5 + [tie] * len(after),
                out_specs=(vm,) * (1 + len(more)),
                compiler_params=params,
                cost_estimate=cost(1),
                name="step_columns",
            )(*given, *after)

        after = () if maps is None else (maps,)
        last = rest.shape[0] == k
        if last:
            here, center_s, center_i = step(0, k, centers, after)
        else:
            here, = step(0, k, (), after)
            rest, center_s, center_i = step(k, rest.shape[0], centers, ())

    half = jax.ShapeDtypeStruct((members, rows_here), BF16)
    state = pl.pallas_call(
        early_kernel,
        out_shape=(shape(members, rows_here), half, half),
        in_specs=[vm] * 2,
        out_specs=(vm,) * 3,
        compiler_params=params,
        cost_estimate=cost(1),
        name="apply_early_maps",
    )(maps, ensemble)
    return pl.pallas_call(
        lambda *refs: final_kernel(batches - 1, slots, *refs),
        out_shape=shape(members, rows_here),
        in_specs=[vm] * 7,
        out_specs=hbm,
        scratch_shapes=[pltpu.VMEM((members, rows_here), F32), pltpu.SemaphoreType.DMA((nb,))],
        compiler_params=params,
        name="apply_maps",
    )(here, swapped, crossed, coef, *state)


def solution(mesh):
    split_specs = P(None, ("gx", "gy"))
    in_specs = (split_specs,) * 5 + (P(), P())
    return jax.shard_map(
        shards, mesh=mesh, in_specs=in_specs, out_specs=split_specs, check_vma=False
    )
```
